128 devices in a mesh: row: 8 (over y, core), col: 16 (over z, x).
Axes of the slice: x: 4, y: 4, z: 4, core: 2. Of those that a mesh axis runs over, the one named last changes fastest.
Arguments:
- pair_count: int32 [2], replicated, may hold values from 2304 to 4608, as said below
- coupling: bfloat16 [2, 4608, 4608], P(None, 'row', 'col'), may hold values from -6 to 6
- amplitudes: bfloat16 [2, 4608, 4608], P(None, 'row', 'col'), may hold values from -0.09375 to 0.09375
- integrals: bfloat16 [2, 4608, 4608], P(None, 'row', 'col'), may hold values from -6 to 6
Outputs:
- cycle_term: bfloat16 [2, 4608, 4608], P(None, 'row', 'col')
The draws below stay inside these ranges and needn't reach their ends.
Inputs may be any that keep to these rules, and one draw needn't show every extreme that they name: `pair_count`: one of the two blocks has exactly 4608 live pairs.
All inputs are finite; a program needn't handle non-finite values.
Results may differ from the reference program's by a relative error of at most 0.0049.
Values may be sent and summed in bfloat16 or wider, within the bound.
A program may use at most 128 MiB of HBM per device.

```python
import jax
import jax.numpy as jnp

PAIRS = 4608
BLOCKS = 2


def draw_pair_count(key, part):
    key = jax.random.fold_in(key, 7)
    first, second = jax.random.split(key)
    other = jax.random.randint(first, (), PAIRS // 2, PAIRS + 1)
    which = jax.random.randint(second, (), 0, 2)
    return jnp.where(jnp.arange(2) == which, PAIRS, other).astype(jnp.int32)


def levels(key, extent, cuts, smallest, top_value):
    gain, own = 1.0, jax.random.fold_in(key, 6)
    for axis_at, blocks in cuts:
        draws = jnp.exp(jax.random.uniform(jax.random.fold_in(own, axis_at), (blocks,), jnp.float32, smallest / len(cuts), top_value / len(cuts)))
        gain = gain * jnp.repeat(draws, extent[axis_at] // blocks).reshape([-1 if axis == axis_at else 1 for axis in range(len(extent))])
    return gain


def gaussian(stream_key, shape, spread, limit, cuts=(), dtype=jnp.bfloat16):
    values = jax.random.normal(stream_key, shape, jnp.float32) * spread
    if len(cuts) > 0:
        values = levels(stream_key, shape, cuts, -0.22, 0.18) * values
    return jnp.clip(values, min=-limit, max=limit).astype(dtype)


def setup_inputs(seed: int = 0) -> dict:
    streams_of = jax.random.split(jax.random.key(seed), 5)
    return {
        "pair_count": draw_pair_count(jax.random.fold_in(streams_of[4], 71), 0),
        "coupling": gaussian(streams_of[1], (BLOCKS, PAIRS, PAIRS), 1.0, 6.0, ((1, 8), (2, 16))),
        "amplitudes": gaussian(streams_of[2], (BLOCKS, PAIRS, PAIRS), PAIRS ** -0.5, 0.09375, ((1, 8), (2, 16))),
        "integrals": gaussian(streams_of[3], (BLOCKS, PAIRS, PAIRS), 1.0, 6.0, ((1, 8), (2, 16))),
    }


def reference(pair_count, coupling, amplitudes, integrals):
    index = jnp.arange(PAIRS)
    results = []
    for block in range(BLOCKS):
        live = index < pair_count[block]
        mask = (live[:, None] & live[None, :]).astype(jnp.bfloat16)
        amps = amplitudes[block] * mask
        coup = coupling[block] * mask
        ints = integrals[block] * mask
        inter = jnp.dot(amps, ints, preferred_element_type=jnp.float32)
        mixed = (coup.astype(jnp.float32) + 0.5 * inter).astype(jnp.bfloat16)
        results.append(jnp.dot(mixed, amps, preferred_element_type=jnp.float32).astype(jnp.bfloat16))
    return jnp.stack(results)
```

```python
import jax
import jax.numpy as jnp
from jax import lax
from jax.experimental import pallas as pl
from jax.experimental.pallas import tpu as pltpu
from jax.sharding import PartitionSpec as P

MESH = pl.DeviceIdType.MESH
F32, BF16 = jnp.float32, jnp.bfloat16
ROWS, COLS = 576, 288
Q = 3
R = ROWS // Q
G = R // 4
PR = 2 * R + G
H = ROWS // 2
RG = 80
PV = 2 * H + RG


def swap4(parts):
    group = lax.broadcasted_iota(jnp.int32, parts[0].shape, 1) // 32
    out = []
    for b in range(4):
        total = None
        for a in range(4):
            v = parts[a] if a == b else pltpu.roll(parts[a], (32 * (a - b)) % 128, 1)
            total = v if total is None else jnp.where(group == a, v, total)
        out.append(total)
    return out


def kernel(
    count, w_hbm, t_hbm, v_hbm, out,
    w_in, t_in, v_in, load_sem,
    ts, tl, tl_s1, tl_r1, tl_s2, tl_r2, tl_sw,
    ws, wp, w_sw,
    vp, vm, vr, vx, v_as, v_ar, v_s1, v_r1, v_s2, v_r2,
    tp, tm, tr, tx, t_as, t_ar, t_s1, t_r1, t_s2, t_r2,
    mb, m_s1, m_r1, m_s2, m_r2,
    lhs1, cs1, own1, d1, d2, d_s1, d_r1, d_s2, d_r2,
    lhs2, cs2, own2, e1, e2, e_s1, e_r1, e_s2, e_r2,
    fo, ob, o_s, o_r,
):
    row, col = lax.axis_index("row"), lax.axis_index("col")
    y, c = row // 2, lax.rem(row, 2)
    z, x = col // 4, lax.rem(col, 4)

    def at(i, n):
        return lax.rem(i + n + 8, 4)

    def dev(dx=0, dy=0, dz=0, core=None):
        return (at(y, dy) * 2 + (c if core is None else core), at(z, dz) * 4 + at(x, dx))

    partner = dev(core=1 - c)
    pending = []

    def send(src, dst, ss, rs, to):
        copy = pltpu.make_async_remote_copy(src, dst, ss, rs, device_id=to, device_id_type=MESH)
        copy.start()
        pending.append(copy)

    def got(dst, rs):
        pltpu.make_async_remote_copy(dst, dst, rs, rs, device_id=partner, device_id_type=MESH).wait_recv()

    loads = [
        pltpu.make_async_copy(a, b, load_sem.at[i])
        for i, (a, b) in enumerate(((v_hbm, v_in), (t_hbm, t_in), (w_hbm, w_in)))
    ]
    for load in loads:
        load.start()
    barrier = pltpu.get_barrier_semaphore()
    friends = [dev(dx=d, core=k) for d in (1, 2, 3) for k in (0, 1)] + [partner]
    friends += [dev(dz=d, core=k) for d in (1, -1) for k in (0, 1)]
    friends += [dev(dy=d) for d in (1, -1)]
    for friend in friends:
        pl.semaphore_signal(barrier, inc=1, device_id=friend, device_id_type=MESH)

    def masked(ref, h, r0, n, c0, w):
        live = count[h]
        rid = row * ROWS + r0 + lax.broadcasted_iota(jnp.int32, (n, w), 0)
        cid = col * COLS + c0 + lax.broadcasted_iota(jnp.int32, (n, w), 1)
        return jnp.where((rid < live) & (cid < live), ref[h, r0 : r0 + n, c0 : c0 + w].astype(F32), 0.0)

    def pack_rows(ref, dst, h, q):
        r0 = q * R
        dst[h, q, 0:R] = masked(ref, h, r0, R, 0, 128).astype(BF16)
        dst[h, q, R : 2 * R] = masked(ref, h, r0, R, 128, 128).astype(BF16)
        strips = [masked(ref, h, r0 + g * G, G, 256, 32) for g in range(4)]
        dst[h, q, 2 * R : PR] = jnp.concatenate(strips, axis=1).astype(BF16)

    def pack_right(ref, dst, h, s):
        r0 = s * H
        dst[h, s, 0:H] = masked(ref, h, r0, H, 0, 128).astype(BF16)
        dst[h, s, H : 2 * H] = masked(ref, h, r0, H, 128, 128).astype(BF16)
        strips = []
        for g in range(4):
            n = min(RG, H - g * RG)
            strip = masked(ref, h, r0 + g * RG, n, 256, 32)
            if n < RG:
                strip = jnp.concatenate([strip, jnp.zeros((RG - n, 32), F32)], axis=0)
            strips.append(strip)
        dst[h, s, 2 * H : PV] = jnp.concatenate(strips, axis=1).astype(BF16)

    def exchange(vp, vm, vx, as_, ar, go):
        for s in range(2):
            tx_ = 2 * c + s
            for h in range(2):
                mine = (tx_ == x) & (c == h)
                to = (y * 2 + h, z * 4 + tx_)
                copies = (
                    (vp.at[h, s, 0 : 2 * H], vm.at[y, x], as_.at[s, h, 0], ar.at[x, 0]),
                    (vp.at[h, s, 2 * H : PV], vx.at[x], as_.at[s, h, 1], ar.at[x, 1]),
                )

                @pl.when(jnp.logical_not(mine))
                def _():
                    for a, b, ss, rs in copies:
                        r = pltpu.make_async_remote_copy(a, b, ss, rs, device_id=to, device_id_type=MESH)
                        if go:
                            r.start()
                        else:
                            r.wait_send()

                if go:

                    @pl.when(mine)
                    def _():
                        for a, b, ss, rs in copies:
                            pltpu.make_async_copy(a, b, rs).start()

    def y_send(vm, vx, vr, ar, s1, r1, o):
        if o < 4:
            xo = at(x, o)
            src = vm.at[y, xo]
            got(src, ar.at[xo, 0])
        else:
            for i in range(4):
                got(vx.at[i], ar.at[i, 1])
            for g, v in enumerate(swap4([vx[i].astype(F32) for i in range(4)])):
                n = min(RG, H - g * RG)
                vr[y, g * RG : g * RG + n] = v[:n].astype(BF16)
            src = vr.at[y]
        for d in (0, 1):
            send(src, src, s1.at[d, o], r1.at[d, o], dev(dy=1 - 2 * d))

    def y_part(vm, vr, k, o, d):
        if o < 4:
            return vm.at[k, at(x, o), pl.ds(d * H, H)]
        return vr.at[k, pl.ds(d * (H // 2), H // 2)]

    def y_all(vm, vr, k, o):
        return vm.at[k, at(x, o)] if o < 4 else vr.at[k]

    def y_forward(vm, vr, r1, s2, r2, o):
        for d in (0, 1):
            k = at(y, 2 * d - 1)
            got(y_all(vm, vr, k, o), r1.at[d, o])
            part = y_part(vm, vr, k, o, d)
            send(part, part, s2.at[d, o], r2.at[d, o], dev(dy=1 - 2 * d))

    def y_last(vm, vr, r2, o):
        for d in (0, 1):
            got(y_part(vm, vr, at(y, 2), o, d), r2.at[d, o])

    def z_forward(buf, r1, s2, r2, q):
        for d in (0, 1):
            k, p = at(z, 2 * d - 1), d * Q + q
            got(buf.at[k, p], r1.at[d, p])
            send(buf.at[k, p], buf.at[k, p], s2.at[d, q], r2.at[d, q], dev(dz=1 - 2 * d))

    def z_last(buf, r1, r2, q):
        for d in (0, 1):
            k, p = at(z, 2 * d - 1), (1 - d) * Q + q
            got(buf.at[k, p], r1.at[d, p])
            got(buf.at[at(z, 2), d * Q + q], r2.at[d, q])

    def make_left(buf, lhs, q):
        for half in (0, 1):
            p, r0 = half * Q + q, half * R
            for k in range(4):
                lhs[q, r0 : r0 + R, k * 256 : k * 256 + 128] = buf[k, p, 0:R]
                lhs[q, r0 : r0 + R, k * 256 + 128 : k * 256 + 256] = buf[k, p, R : 2 * R]
            for g, v in enumerate(swap4([buf[k, p, 2 * R : PR].astype(F32) for k in range(4)])):
                lhs[q, r0 + g * G : r0 + g * G + G, 1024:1152] = v.astype(BF16)

    def dot_main(lhs, vm, cs, own, q, o):
        t = at(x, o)
        big = [jnp.concatenate([vm[k, t, 0:256], vm[k, t, H : H + 256]], axis=1) for k in range(4)]
        small = [jnp.concatenate([vm[k, t, 256:H], vm[k, t, H + 256 : 2 * H]], axis=1) for k in range(4)]
        part = jnp.dot(lhs[q], jnp.concatenate(big + small, axis=0), preferred_element_type=F32)
        for half in (0, 1):
            p = half * Q + q
            for lane in (0, 1):
                v = part[half * R : half * R + R, lane * 128 : lane * 128 + 128]
                if o == 0:
                    own[p, lane * R : lane * R + R] = v
                else:
                    cs[o - 1, p, lane * R : lane * R + R] = v.astype(BF16)

    def dot_rest(lhs, vr, cs, own, q):
        right = jnp.concatenate([vr[k, 0:256] for k in range(4)] + [vr[k, 256:H] for k in range(4)], axis=0)
        part = jnp.dot(lhs[q], right, preferred_element_type=F32)
        for half in (0, 1):
            p = half * Q + q
            by_x = swap4([part[half * R + g * G : half * R + g * G + G] for g in range(4)])
            for o in range(4):
                t = at(x, o)
                v = jnp.where(t == 0, by_x[0], jnp.where(t == 1, by_x[1], jnp.where(t == 2, by_x[2], by_x[3])))
                if o == 0:
                    own[p, 2 * R : PR] = v
                else:
                    cs[o - 1, p, 2 * R : PR] = v.astype(BF16)

    def first_hop(cs, d1, s1, r1, q):
        for d in (0, 1):
            send(cs.at[1, d * Q + q], d1.at[d, q], s1.at[d, q], r1.at[d, q], dev(dx=1 - 2 * d))

    def alone(cs, d2, s2, r2, q, d):
        p = (1 - d) * Q + q
        send(cs.at[2 * d, p], d2.at[d, p], s2.at[d, p], r2.at[d, p], dev(dx=1 - 2 * d))

    def relay(cs, d1, d2, r1, s2, r2, q):
        for d in (0, 1):
            p = d * Q + q
            got(d1.at[d, q], r1.at[d, q])
            cs[2 * d, p] = (cs[2 * d, p].astype(F32) + d1[d, q].astype(F32)).astype(BF16)
            send(cs.at[2 * d, p], d2.at[d, p], s2.at[d, p], r2.at[d, p], dev(dx=1 - 2 * d))

    def total(own, d2, r2, p):
        for d in (0, 1):
            got(d2.at[d, p], r2.at[d, p])
        return own[p] + d2[0, p].astype(F32) + d2[1, p].astype(F32)

    def mix(q):
        for half in (0, 1):
            p = half * Q + q
            mb[z, p] = (wp[p].astype(F32) + 0.5 * total(own1, d2, d_r2, p)).astype(BF16)
            for d in (0, 1):
                send(mb.at[z, p], mb.at[z, p], m_s1.at[d, p], m_r1.at[d, p], dev(dz=1 - 2 * d))

    def unpack(v, h, q):
        r0 = q * R
        out[h, r0 : r0 + R, 0:128] = v[0:R].astype(BF16)
        out[h, r0 : r0 + R, 128:256] = v[R : 2 * R].astype(BF16)
        for g in range(4):
            strip = v[2 * R : PR]
            if g:
                strip = pltpu.roll(strip, 128 - 32 * g, 1)
            out[h, r0 + g * G : r0 + g * G + G, 256:288] = strip[:, 0:32].astype(BF16)

    def finish(q):
        for half in (0, 1):
            fo[half, q] = total(own2, e2, e_r2, half * Q + q).astype(BF16)
        send(fo.at[1 - c, q], ob.at[q], o_s.at[q], o_r.at[q], partner)
        unpack(fo[c, q].astype(F32), c, q)

    def collect(q):
        got(ob.at[q], o_r.at[q])
        unpack(ob[q].astype(F32), 1 - c, q)

    V = dict(vm=vm, vr=vr)
    T = dict(vm=tm, vr=tr)

    def yv_send(o):
        y_send(vm, vx, vr, v_ar, v_s1, v_r1, o)

    def yv_fwd(o):
        y_forward(vm, vr, v_r1, v_s2, v_r2, o)

    def yt_send(o):
        y_send(tm, tx, tr, t_ar, t_s1, t_r1, o)

    def yt_fwd(o):
        y_forward(tm, tr, t_r1, t_s2, t_r2, o)

    loads[0].wait()
    for h in range(2):
        for s in range(2):
            pack_right(v_in, vp, h, s)
    pl.semaphore_wait(barrier, len(friends))
    exchange(vp, vm, vx, v_as, v_ar, True)
    loads[1].wait()
    for q in range(Q):
        for h in range(2):
            pack_rows(t_in, ts, h, q)
            for d in (0, 1):
                send(ts.at[h, q], tl.at[z, c * Q + q], tl_s1.at[d, h, q], tl_r1.at[d, c * Q + q], dev(dz=1 - 2 * d, core=h))
        send(ts.at[1 - c, q], tl.at[z, c * Q + q], tl_sw.at[0, q], tl_sw.at[1, q], partner)
        tl[z, c * Q + q] = ts[c, q]
    yv_send(0)
    for h in range(2):
        for s in range(2):
            pack_right(t_in, tp, h, s)
    exchange(tp, tm, tx, t_as, t_ar, True)
    loads[2].wait()
    for h in range(2):
        for q in range(Q):
            pack_rows(w_in, ws, h, q)
    send(ws.at[1 - c], wp.at[pl.ds(c * Q, Q)], w_sw.at[0], w_sw.at[1], partner)
    for q in range(Q):
        wp[c * Q + q] = ws[c, q]
    yv_send(2)
    z_forward(tl, tl_r1, tl_s2, tl_r2, 0)
    yv_fwd(0)
    yv_send(4)
    yv_send(1)
    yv_send(3)
    yv_fwd(2)
    z_forward(tl, tl_r1, tl_s2, tl_r2, 1)
    yv_fwd(4)

    def left_ready(q):
        z_last(tl, tl_r1, tl_r2, q)
        got(tl.at[z, (1 - c) * Q + q], tl_sw.at[1, q])
        make_left(tl, lhs1, q)

    left_ready(0)
    y_last(vm, vr, v_r2, 2)
    y_last(vm, vr, v_r2, 4)
    dot_rest(lhs1, vr, cs1, own1, 0)
    dot_main(lhs1, vm, cs1, own1, 0, 2)
    first_hop(cs1, d1, d_s1, d_r1, 0)
    z_forward(tl, tl_r1, tl_s2, tl_r2, 2)
    yv_fwd(1)
    yv_fwd(3)
    left_ready(1)
    dot_rest(lhs1, vr, cs1, own1, 1)
    dot_main(lhs1, vm, cs1, own1, 1, 2)
    first_hop(cs1, d1, d_s1, d_r1, 1)
    y_last(vm, vr, v_r2, 1)
    dot_main(lhs1, vm, cs1, own1, 0, 1)
    alone(cs1, d2, d_s2, d_r2, 0, 0)
    y_last(vm, vr, v_r2, 3)
    dot_main(lhs1, vm, cs1, own1, 0, 3)
    alone(cs1, d2, d_s2, d_r2, 0, 1)
    relay(cs1, d1, d2, d_r1, d_s2, d_r2, 0)
    for o in (2, 4, 1, 3, 0):
        yt_send(o)
    y_last(vm, vr, v_r2, 0)
    dot_main(lhs1, vm, cs1, own1, 0, 0)
    left_ready(2)
    dot_rest(lhs1, vr, cs1, own1, 2)
    dot_main(lhs1, vm, cs1, own1, 2, 2)
    first_hop(cs1, d1, d_s1, d_r1, 2)
    for q in (1, 2):
        dot_main(lhs1, vm, cs1, own1, q, 1)
        alone(cs1, d2, d_s2, d_r2, q, 0)
        dot_main(lhs1, vm, cs1, own1, q, 3)
        alone(cs1, d2, d_s2, d_r2, q, 1)
        relay(cs1, d1, d2, d_r1, d_s2, d_r2, q)
        dot_main(lhs1, vm, cs1, own1, q, 0)
    yt_fwd(2)
    got(wp.at[pl.ds((1 - c) * Q, Q)], w_sw.at[1])
    mix(0)
    yt_fwd(4)
    mix(1)
    yt_fwd(1)
    mix(2)
    yt_fwd(3)

    def mixed_ready(q):
        z_last(mb, m_r1, m_r2, q)
        make_left(mb, lhs2, q)

    z_forward(mb, m_r1, m_s2, m_r2, 0)
    yt_fwd(0)
    z_forward(mb, m_r1, m_s2, m_r2, 1)
    mixed_ready(0)
    y_last(tm, tr, t_r2, 2)
    y_last(tm, tr, t_r2, 4)
    dot_rest(lhs2, tr, cs2, own2, 0)
    dot_main(lhs2, tm, cs2, own2, 0, 2)
    first_hop(cs2, e1, e_s1, e_r1, 0)
    y_last(tm, tr, t_r2, 1)
    dot_main(lhs2, tm, cs2, own2, 0, 1)
    alone(cs2, e2, e_s2, e_r2, 0, 0)
    y_last(tm, tr, t_r2, 3)
    dot_main(lhs2, tm, cs2, own2, 0, 3)
    alone(cs2, e2, e_s2, e_r2, 0, 1)
    z_forward(mb, m_r1, m_s2, m_r2, 2)
    y_last(tm, tr, t_r2, 0)
    for q in (1, 2):
        mixed_ready(q)
        dot_rest(lhs2, tr, cs2, own2, q)
        dot_main(lhs2, tm, cs2, own2, q, 2)
        first_hop(cs2, e1, e_s1, e_r1, q)
        relay(cs2, e1, e2, e_r1, e_s2, e_r2, q - 1)
        dot_main(lhs2, tm, cs2, own2, q, 1)
        alone(cs2, e2, e_s2, e_r2, q, 0)
        dot_main(lhs2, tm, cs2, own2, q, 3)
        alone(cs2, e2, e_s2, e_r2, q, 1)
        dot_main(lhs2, tm, cs2, own2, q - 1, 0)
        if q == 2:
            finish(0)
    relay(cs2, e1, e2, e_r1, e_s2, e_r2, 2)
    dot_main(lhs2, tm, cs2, own2, 2, 0)
    finish(1)
    collect(0)
    finish(2)
    collect(1)
    collect(2)
    exchange(vp, vm, vx, v_as, v_ar, False)
    exchange(tp, tm, tx, t_as, t_ar, False)
    for copy in pending:
        copy.wait_send()


def per_device(pair_count, coupling, amplitudes, integrals):
    dma = pltpu.SemaphoreType.DMA
    shard = coupling.shape

    def piece(*lead, dtype=BF16):
        return pltpu.VMEM((*lead, PR, 128), dtype)

    def right():
        return [
            pltpu.VMEM((2, 2, PV, 128), BF16), pltpu.VMEM((4, 4, 2 * H, 128), BF16), pltpu.VMEM((4, H, 128), BF16),
            pltpu.VMEM((4, RG, 128), BF16), dma((2, 2, 2)), dma((4, 2)),
            dma((2, 5)), dma((2, 5)), dma((2, 5)), dma((2, 5)),
        ]

    def sums():
        return [
            pltpu.VMEM((Q, 2 * R, 1152), BF16), piece(3, 2 * Q), piece(2 * Q, dtype=F32), piece(2, Q), piece(2, 2 * Q),
            dma((2, Q)), dma((2, Q)), dma((2, 2 * Q)), dma((2, 2 * Q)),
        ]

    scratch = [pltpu.VMEM(shard, BF16)] * 3 + [dma((3,))]
    scratch += [piece(2, Q), piece(4, 2 * Q), dma((2, 2, Q)), dma((2, 2 * Q)), dma((2, Q)), dma((2, Q)), dma((2, Q))]
    scratch += [piece(2, Q), piece(2 * Q), dma((2,))]
    scratch += right() + right()
    scratch += [piece(4, 2 * Q), dma((2, 2 * Q)), dma((2, 2 * Q)), dma((2, Q)), dma((2, Q))]
    scratch += sums() + sums()
    scratch += [piece(2, Q), piece(Q), dma((Q,)), dma((Q,))]
    return pl.pallas_call(
        kernel,
        out_shape=jax.ShapeDtypeStruct(shard, BF16),
        in_specs=[pl.BlockSpec(memory_space=pltpu.SMEM)] + [pl.BlockSpec(memory_space=pl.ANY)] * 3,
        out_specs=pl.BlockSpec(memory_space=pltpu.VMEM),
        scratch_shapes=scratch,
        compiler_params=pltpu.CompilerParams(collective_id=0, has_side_effects=True, vmem_limit_bytes=56 << 20),
        cost_estimate=pl.CostEstimate(flops=6115295232, bytes_accessed=2654208, transcendentals=0),
        name="cycle",
    )(pair_count, coupling, amplitudes, integrals)


def solution(mesh):
    split = P(None, "row", "col")
    return jax.shard_map(per_device, mesh=mesh, in_specs=(P(), split, split, split), out_specs=split, check_vma=False)
```

```python
from typing import Any, NamedTuple

import jax
import jax.numpy as jnp
from jax import lax
from jax.experimental import pallas as pl
from jax.experimental.pallas import tpu as pltpu
from jax.sharding import PartitionSpec as P

MESH = pl.DeviceIdType.MESH
F32, BF16 = jnp.float32, jnp.bfloat16
ROWS, COLS = 576, 288
Q = 3
R = ROWS // Q
G = R // 4
PR = 2 * R + G
H = ROWS // 2
RG = 80
PV = 2 * H + RG


def swap4(parts):
    group = lax.broadcasted_iota(jnp.int32, parts[0].shape, 1) // 32
    out = []
    for b in range(4):
        total = None
        for a in range(4):
            v = parts[a] if a == b else pltpu.roll(parts[a], (32 * (a - b)) % 128, 1)
            total = v if total is None else jnp.where(group == a, v, total)
        out.append(total)
    return out

SCHEDULE = (
    ("b",), ("p", 1), ("v", 1), ("p", 0), ("v", 0), ("pt",), ("r", 0), ("r", 1), ("t", 0), ("vs", 1), ("vs", 2),
    ("vs", 4), ("t", 1), ("lf", 0), ("vs", 3), ("t", 2), ("lf", 1), ("vf", 2), ("vf", 4), ("vf", 1), ("l", 0),
    ("l", 1), ("lf", 2), ("vf", 3), ("dr", 1, 0), ("vs", 0), ("w",), ("d", 1, 0, 2), ("dr", 1, 1), ("l", 2),
    ("d", 1, 0, 1), ("ts", 2), ("d", 1, 1, 2), ("d", 1, 0, 3), ("re", 1, 0), ("vf", 0), ("d", 1, 1, 3),
    ("d", 1, 1, 1), ("dr", 1, 2), ("d", 1, 2, 2), ("d", 1, 2, 3), ("ts", 4), ("d", 1, 2, 1), ("re", 1, 1),
    ("ts", 1), ("d", 1, 0, 0), ("mix", 0), ("ts", 3), ("re", 1, 2), ("tf", 4), ("tf", 2), ("d", 1, 1, 0),
    ("mix", 1), ("ts", 0), ("mf", 0), ("d", 1, 2, 0), ("mix", 2), ("mf", 1), ("tf", 1), ("m", 0), ("tf", 3),
    ("dr", 2, 0), ("d", 2, 0, 2), ("mf", 2), ("m", 1), ("dr", 2, 1), ("d", 2, 1, 2), ("tf", 0), ("d", 2, 0, 1),
    ("d", 2, 0, 3), ("re", 2, 0), ("m", 2), ("dr", 2, 2), ("d", 2, 2, 2), ("d", 2, 1, 1), ("d", 2, 0, 0),
    ("d", 2, 2, 3), ("d", 2, 1, 0), ("d", 2, 1, 3), ("d", 2, 2, 0), ("d", 2, 2, 1), ("re", 2, 1), ("fin", 0),
    ("re", 2, 2), ("fin", 1), ("fin", 2), ("col", 0), ("col", 1), ("col", 2),
)


def kernel(
    count, w_hbm, t_hbm, v_hbm, out,
    w_in, t_in, v_in, load_sem, live,
    w_t, t_t, v_t,
    ts, tl, tl_s1, tl_r1, tl_s2, tl_r2, tl_sw,
    ws, wp, w_sw,
    vp, vm, vr, vx, v_as, v_ar, v_s1, v_r1, v_s2, v_r2,
    tp, tm, tr, tx, t_as, t_ar, t_s1, t_r1, t_s2, t_r2,
    mb, m_s1, m_r1, m_s2, m_r2,
    lhs1, cs1, own1, d1, d2, d_s1, d_r1, d_s2, d_r2,
    lhs2, cs2, own2, e1, e2, e_s1, e_r1, e_s2, e_r2,
    fo, ob, o_t, o_s, o_r,
):
    row, col = lax.axis_index("row"), lax.axis_index("col")
    y, c = row // 2, lax.rem(row, 2)
    z, x = col // 4, lax.rem(col, 4)
    a, b = jnp.where(c == 0, z, x), jnp.where(c == 0, x, z)

    def at(i, n):
        return lax.rem(i + n + 8, 4)

    def dev(dx=0, dy=0, dz=0, core=None):
        return (at(y, dy) * 2 + (c if core is None else core), at(z, dz) * 4 + at(x, dx))

    def ring(n):
        return (row, jnp.where(c == 0, at(z, n) * 4 + x, z * 4 + at(x, n)))

    def line(n):
        return (row, jnp.where(c == 0, z * 4 + at(x, n), at(z, n) * 4 + x))

    partner = dev(core=1 - c)
    pending = []

    def remote(src, dst, ss, rs, to):
        return pltpu.make_async_remote_copy(src, dst, ss, rs, device_id=to, device_id_type=MESH)

    def send(src, dst, ss, rs, to):
        copy = remote(src, dst, ss, rs, to)
        copy.start()
        pending.append(copy)

    def got(dst, rs):
        remote(dst, dst, rs, rs, partner).wait_recv()

    loads = [
        pltpu.make_async_copy(s, d, load_sem.at[i])
        for i, (s, d) in enumerate(((v_hbm, v_in), (t_hbm, t_in), (w_hbm, w_in)))
    ]
    for load in loads:
        load.start()
    barrier = pltpu.get_barrier_semaphore()
    friends = [partner] + [dev(dx=n, core=k) for n in (1, 2, 3) for k in (0, 1)]
    friends += [dev(dz=n, core=k) for n in (1, -1) for k in (0, 1)] + [dev(dy=n) for n in (1, -1)]
    for friend in friends:
        pl.semaphore_signal(barrier, inc=1, device_id=friend, device_id_type=MESH)
    for n in range(4):
        core = y // 2

        @pl.when((c == 1) & jnp.logical_not((n == z) & (y == z) & (core == 1)))
        def _():
            source = (z * 2 + core, n * 4 + x)
            pl.semaphore_signal(barrier, inc=1, device_id=source, device_id_type=MESH)

    greetings = len(friends) + 2 - jnp.where((c == 1) & (y == z) & (y >= 2), 1, 0)
    for h in range(2):
        cid = col * COLS + lax.broadcasted_iota(jnp.int32, (COLS, ROWS), 0)
        rid = row * ROWS + lax.broadcasted_iota(jnp.int32, (COLS, ROWS), 1)
        live[h] = jnp.where((rid < count[h]) & (cid < count[h]), 1.0, 0.0).astype(BF16)

    def turn(src, dst, h):
        dst[h] = jnp.transpose(src[h] * live[h])

    def pack_rows(ref, dst, h, q):
        r0 = q * R
        dst[h, q, 0:R] = ref[h, r0 : r0 + R, 0:128]
        dst[h, q, R : 2 * R] = ref[h, r0 : r0 + R, 128:256]
        strips = [ref[h, r0 + g * G : r0 + g * G + G, 256:288].astype(F32) for g in range(4)]
        dst[h, q, 2 * R : PR] = jnp.concatenate(strips, axis=1).astype(BF16)

    def pack_right(ref, dst, h, s):
        r0 = s * H
        dst[h, s, 0:H] = ref[h, r0 : r0 + H, 0:128]
        dst[h, s, H : 2 * H] = ref[h, r0 : r0 + H, 128:256]
        strips = []
        for g in range(4):
            n = min(RG, H - g * RG)
            strip = ref[h, r0 + g * RG : r0 + g * RG + n, 256:288].astype(F32)
            if n < RG:
                strip = jnp.concatenate([strip, jnp.zeros((RG - n, 32), F32)], axis=0)
            strips.append(strip)
        dst[h, s, 2 * H : PV] = jnp.concatenate(strips, axis=1).astype(BF16)

    def either(mine, copies, to, go):
        @pl.when(jnp.logical_not(mine))
        def _():
            for copy in copies:
                if go:
                    remote(*copy, to).start()
                else:
                    remote(*copy, to).wait_send()

        if go:

            @pl.when(mine)
            def _():
                for src, dst, _, rs in copies:
                    pltpu.make_async_copy(src, dst, rs).start()

    def exchange(ops, h, go):
        for s in range(2):
            to = 2 * c + s
            k, n = (y, x) if h == 0 else (to, z)
            copies = (
                (ops.p.at[h, s, 0 : 2 * H], ops.m.at[k, n], ops.as_.at[s, h, 0], ops.ar.at[n, 0]),
                (ops.p.at[h, s, 2 * H : PV], ops.x.at[n], ops.as_.at[s, h, 1], ops.ar.at[n, 1]),
            )
            if h == 0:
                either((to == x) & (c == 0), copies, (y * 2, z * 4 + to), go)
            else:
                either((to == y) & (y == z) & (c == 1), copies, (to * 2 + 1, y * 4 + x), go)

    def y_send(ops, o):
        if o < 4:
            src = ops.m.at[y, at(b, o)]
            got(src, ops.ar.at[at(b, o), 0])
        else:
            for i in range(4):
                got(ops.x.at[i], ops.ar.at[i, 1])
            for g, v in enumerate(swap4([ops.x[i].astype(F32) for i in range(4)])):
                n = min(RG, H - g * RG)
                ops.r[y, g * RG : g * RG + n] = v[:n].astype(BF16)
            src = ops.r.at[y]
        for d in (0, 1):
            send(src, src, ops.s1.at[d, o], ops.r1.at[d, o], dev(dy=1 - 2 * d))

    def y_part(ops, k, o, d):
        if o < 4:
            return ops.m.at[k, at(b, o), pl.ds(d * H, H)]
        return ops.r.at[k, pl.ds(d * (H // 2), H // 2)]

    def y_forward(ops, o):
        for d in (0, 1):
            k = at(y, 2 * d - 1)
            got(ops.m.at[k, at(b, o)] if o < 4 else ops.r.at[k], ops.r1.at[d, o])
            part = y_part(ops, k, o, d)
            send(part, part, ops.s2.at[d, o], ops.r2.at[d, o], dev(dy=1 - 2 * d))

    def y_last(ops, o):
        for d in (0, 1):
            got(y_part(ops, at(y, 2), o, d), ops.r2.at[d, o])

    def ring_forward(buf, r1, s2, r2, q):
        for d in (0, 1):
            k, p = at(a, 2 * d - 1), d * Q + q
            got(buf.at[k, p], r1.at[d, p])
            send(buf.at[k, p], buf.at[k, p], s2.at[d, q], r2.at[d, q], ring(1 - 2 * d))

    def ring_last(buf, r1, r2, q):
        for d in (0, 1):
            k, p = at(a, 2 * d - 1), (1 - d) * Q + q
            got(buf.at[k, p], r1.at[d, p])
            got(buf.at[at(a, 2), d * Q + q], r2.at[d, q])

    def make_left(buf, lhs, q):
        for half in (0, 1):
            p, r0 = half * Q + q, half * R
            for k in range(4):
                lhs[q, r0 : r0 + R, k * 256 : k * 256 + 128] = buf[k, p, 0:R]
                lhs[q, r0 : r0 + R, k * 256 + 128 : k * 256 + 256] = buf[k, p, R : 2 * R]
            for g, v in enumerate(swap4([buf[k, p, 2 * R : PR].astype(F32) for k in range(4)])):
                lhs[q, r0 + g * G : r0 + g * G + G, 1024:1152] = v.astype(BF16)

    def dot_rest(st, q):
        vr = st.ops.r
        y_last(st.ops, 4) if q == 0 else None
        right = jnp.concatenate([vr[k, 0:256] for k in range(4)] + [vr[k, 256:H] for k in range(4)], axis=0)
        part = jnp.dot(st.lhs[q], right, preferred_element_type=F32)
        for half in (0, 1):
            p = half * Q + q
            by = swap4([part[half * R + g * G : half * R + g * G + G] for g in range(4)])
            for o in range(4):
                t = at(b, o)
                v = jnp.where(t == 0, by[0], jnp.where(t == 1, by[1], jnp.where(t == 2, by[2], by[3])))
                if o == 0:
                    st.own[p, 2 * R : PR] = v
                else:
                    st.cs[o - 1, p, 2 * R : PR] = v.astype(BF16)

    def dot_main(st, q, o):
        vm, t = st.ops.m, at(b, o)
        y_last(st.ops, o) if q == 0 else None
        big = [jnp.concatenate([vm[k, t, 0:256], vm[k, t, H : H + 256]], axis=1) for k in range(4)]
        small = [jnp.concatenate([vm[k, t, 256:H], vm[k, t, H + 256 : 2 * H]], axis=1) for k in range(4)]
        part = jnp.dot(st.lhs[q], jnp.concatenate(big + small, axis=0), preferred_element_type=F32)
        for half in (0, 1):
            p = half * Q + q
            for lane in (0, 1):
                v = part[half * R : half * R + R, lane * 128 : lane * 128 + 128]
                if o == 0:
                    st.own[p, lane * R : lane * R + R] = v
                else:
                    st.cs[o - 1, p, lane * R : lane * R + R] = v.astype(BF16)
        if o == 2:
            for d in (0, 1):
                send(st.cs.at[1, d * Q + q], st.l1.at[d, q], st.s1.at[d, q], st.r1.at[d, q], line(1 - 2 * d))
        elif o:
            d = o // 2
            p = (1 - d) * Q + q
            send(st.cs.at[2 * d, p], st.l2.at[d, p], st.s2.at[d, p], st.r2.at[d, p], line(1 - 2 * d))

    def relay(st, q):
        for d in (0, 1):
            p = d * Q + q
            got(st.l1.at[d, q], st.r1.at[d, q])
            st.cs[2 * d, p] = (st.cs[2 * d, p].astype(F32) + st.l1[d, q].astype(F32)).astype(BF16)
            send(st.cs.at[2 * d, p], st.l2.at[d, p], st.s2.at[d, p], st.r2.at[d, p], line(1 - 2 * d))

    def total(st, p):
        for d in (0, 1):
            got(st.l2.at[d, p], st.r2.at[d, p])
        return st.own[p] + st.l2[0, p].astype(F32) + st.l2[1, p].astype(F32)

    def unpack(v, h, q):
        r0 = q * R
        o_t[h, r0 : r0 + R, 0:128] = v[0:R].astype(BF16)
        o_t[h, r0 : r0 + R, 128:256] = v[R : 2 * R].astype(BF16)
        for g in range(4):
            strip = v[2 * R : PR]
            if g:
                strip = pltpu.roll(strip, 128 - 32 * g, 1)
            o_t[h, r0 + g * G : r0 + g * G + G, 256:288] = strip[:, 0:32].astype(BF16)

    def turn_back(h, q):
        if q == 1:
            out[h, :, 0:384] = jnp.transpose(o_t[h, 0:384])
        if q == 2:
            out[h, :, 384:576] = jnp.transpose(o_t[h, 384:576])

    v_ops = Ops(vp, vm, vr, vx, v_as, v_ar, v_s1, v_r1, v_s2, v_r2)
    t_ops = Ops(tp, tm, tr, tx, t_as, t_ar, t_s1, t_r1, t_s2, t_r2)
    stages = {
        1: Stage(v_ops, lhs1, cs1, own1, d1, d2, d_s1, d_r1, d_s2, d_r2),
        2: Stage(t_ops, lhs2, cs2, own2, e1, e2, e_s1, e_r1, e_s2, e_r2),
    }

    def step_p(h):
        if h == 1:
            loads[0].wait()
        turn(v_in, v_t, h)
        for s in range(2):
            pack_right(v_t, vp, h, s)

    def step_b():
        pl.semaphore_wait(barrier, greetings)

    def step_v(h):
        exchange(v_ops, h, True)

    def step_pt():
        loads[1].wait()
        for h in range(2):
            turn(t_in, t_t, h)
            for q in range(Q):
                pack_rows(t_t, ts, h, q)
        for q in range(Q):
            tl[a, c * Q + q] = ts[c, q]

    def step_t(q):
        for h in range(2):
            for d in (0, 1):
                to = dev(dz=1 - 2 * d, core=0) if h == 0 else dev(dx=1 - 2 * d, core=1)
                place = z if h == 0 else x
                send(ts.at[h, q], tl.at[place, c * Q + q], tl_s1.at[d, h, q], tl_r1.at[d, c * Q + q], to)
        send(ts.at[1 - c, q], tl.at[b, c * Q + q], tl_sw.at[0, q], tl_sw.at[1, q], partner)

    def step_r(h):
        for s in range(2):
            pack_right(t_t, tp, h, s)
        exchange(t_ops, h, True)

    def step_w():
        loads[2].wait()
        for h in range(2):
            turn(w_in, w_t, h)
            for q in range(Q):
                pack_rows(w_t, ws, h, q)
        send(ws.at[1 - c], wp.at[pl.ds(c * Q, Q)], w_sw.at[0], w_sw.at[1], partner)
        for q in range(Q):
            wp[c * Q + q] = ws[c, q]

    def step_left(q):
        ring_last(tl, tl_r1, tl_r2, q)
        got(tl.at[a, (1 - c) * Q + q], tl_sw.at[1, q])
        make_left(tl, lhs1, q)

    def step_mix(q):
        if q == 0:
            got(wp.at[pl.ds((1 - c) * Q, Q)], w_sw.at[1])
        for half in (0, 1):
            p = half * Q + q
            mb[a, p] = (wp[p].astype(F32) + 0.5 * total(stages[1], p)).astype(BF16)
            for d in (0, 1):
                send(mb.at[a, p], mb.at[a, p], m_s1.at[d, p], m_r1.at[d, p], ring(1 - 2 * d))

    def step_mixed(q):
        ring_last(mb, m_r1, m_r2, q)
        make_left(mb, lhs2, q)

    def step_finish(q):
        for half in (0, 1):
            fo[half, q] = total(stages[2], half * Q + q).astype(BF16)
        send(fo.at[1 - c, q], ob.at[q], o_s.at[q], o_r.at[q], partner)
        unpack(fo[c, q].astype(F32), c, q)
        turn_back(c, q)

    def step_collect(q):
        got(ob.at[q], o_r.at[q])
        unpack(ob[q].astype(F32), 1 - c, q)
        turn_back(1 - c, q)

    steps = {
        "v": step_v, "t": step_t, "r": step_r, "w": step_w,
        "p": step_p, "b": step_b, "pt": step_pt,
        "vs": lambda o: y_send(v_ops, o), "vf": lambda o: y_forward(v_ops, o),
        "ts": lambda o: y_send(t_ops, o), "tf": lambda o: y_forward(t_ops, o),
        "lf": lambda q: ring_forward(tl, tl_r1, tl_s2, tl_r2, q), "l": step_left,
        "mf": lambda q: ring_forward(mb, m_r1, m_s2, m_r2, q), "m": step_mixed,
        "dr": lambda s, q: dot_rest(stages[s], q), "d": lambda s, q, o: dot_main(stages[s], q, o),
        "re": lambda s, q: relay(stages[s], q), "mix": step_mix,
        "fin": step_finish, "col": step_collect,
    }
    for step in SCHEDULE:
        steps[step[0]](*step[1:])
    for ops in (v_ops, t_ops):
        for h in (0, 1):
            exchange(ops, h, False)
    for copy in pending:
        copy.wait_send()


class Ops(NamedTuple):
    p: Any
    m: Any
    r: Any
    x: Any
    as_: Any
    ar: Any
    s1: Any
    r1: Any
    s2: Any
    r2: Any


class Stage(NamedTuple):
    ops: Any
    lhs: Any
    cs: Any
    own: Any
    l1: Any
    l2: Any
    s1: Any
    r1: Any
    s2: Any
    r2: Any


def per_device(pair_count, coupling, amplitudes, integrals):
    dma = pltpu.SemaphoreType.DMA
    coupling, amplitudes, integrals = (jnp.transpose(v, (0, 2, 1)) for v in (coupling, amplitudes, integrals))
    turned, shard = (2, COLS, ROWS), (2, ROWS, COLS)

    def piece(*lead, dtype=BF16):
        return pltpu.VMEM((*lead, PR, 128), dtype)

    def right():
        return [
            pltpu.VMEM((2, 2, PV, 128), BF16), pltpu.VMEM((4, 4, 2 * H, 128), BF16), pltpu.VMEM((4, H, 128), BF16),
            pltpu.VMEM((4, RG, 128), BF16), dma((2, 2, 2)), dma((4, 2)),
            dma((2, 5)), dma((2, 5)), dma((2, 5)), dma((2, 5)),
        ]

    def sums():
        return [
            pltpu.VMEM((Q, 2 * R, 1152), BF16), piece(3, 2 * Q), piece(2 * Q, dtype=F32), piece(2, Q), piece(2, 2 * Q),
            dma((2, Q)), dma((2, Q)), dma((2, 2 * Q)), dma((2, 2 * Q)),
        ]

    scratch = [pltpu.VMEM(turned, BF16)] * 3 + [dma((3,)), pltpu.VMEM(turned, BF16)] + [pltpu.VMEM(shard, BF16)] * 3
    scratch += [piece(2, Q), piece(4, 2 * Q), dma((2, 2, Q)), dma((2, 2 * Q)), dma((2, Q)), dma((2, Q)), dma((2, Q))]
    scratch += [piece(2, Q), piece(2 * Q), dma((2,))]
    scratch += right() + right()
    scratch += [piece(4, 2 * Q), dma((2, 2 * Q)), dma((2, 2 * Q)), dma((2, Q)), dma((2, Q))]
    scratch += sums() + sums()
    scratch += [piece(2, Q), piece(Q), pltpu.VMEM(shard, BF16), dma((Q,)), dma((Q,))]
    result = pl.pallas_call(
        kernel,
        out_shape=jax.ShapeDtypeStruct(turned, BF16),
        in_specs=[pl.BlockSpec(memory_space=pltpu.SMEM)] + [pl.BlockSpec(memory_space=pl.ANY)] * 3,
        out_specs=pl.BlockSpec(memory_space=pltpu.VMEM),
        scratch_shapes=scratch,
        compiler_params=pltpu.CompilerParams(collective_id=0, has_side_effects=True, vmem_limit_bytes=56 << 20),
        cost_estimate=pl.CostEstimate(flops=6115295232, bytes_accessed=2654208, transcendentals=0),
        name="cycle",
    )(pair_count, coupling, amplitudes, integrals)
    return jnp.transpose(result, (0, 2, 1))


def solution(mesh):
    split = P(None, "row", "col")
    return jax.shard_map(per_device, mesh=mesh, in_specs=(P(), split, split, split), out_specs=split, check_vma=False)
```

```python
from typing import Any, NamedTuple

import jax
import jax.numpy as jnp
from jax import lax
from jax.experimental import pallas as pl
from jax.experimental.pallas import tpu as pltpu
from jax.sharding import PartitionSpec as P

MESH = pl.DeviceIdType.MESH
F32, BF16 = jnp.float32, jnp.bfloat16
ROWS, COLS = 576, 288
Q = 3
R = ROWS // Q
G = R // 4
PR = 2 * R + G
H = ROWS // 2
RG = 80
PV = 2 * H + RG


def swap4(parts):
    group = lax.broadcasted_iota(jnp.int32, parts[0].shape, 1) // 32
    out = []
    for b in range(4):
        total = None
        for a in range(4):
            v = parts[a] if a == b else pltpu.roll(parts[a], (32 * (a - b)) % 128, 1)
            total = v if total is None else jnp.where(group == a, v, total)
        out.append(total)
    return out

SCHEDULE = (
    ("p", 1), ("b",), ("v", 1), ("p", 0), ("v", 0), ("pt",), ("r", 1), ("vs", 2), ("t", 0), ("vs", 1), ("vs", 4),
    ("t", 1), ("t", 2), ("lf", 0), ("vs", 3), ("lf", 2), ("vf", 4), ("w",), ("lf", 1), ("vf", 2), ("vf", 1),
    ("r", 0), ("l", 0), ("vf", 3), ("vs", 0), ("l", 2), ("dr", 1, 0), ("dr", 1, 2), ("l", 1), ("d", 1, 0, 2),
    ("d", 1, 2, 2), ("dr", 1, 1), ("d", 1, 1, 2), ("ts", 2), ("d", 1, 0, 1), ("d", 1, 0, 3), ("d", 1, 1, 3),
    ("d", 1, 2, 1), ("vf", 0), ("re", 1, 0), ("ts", 4), ("ts", 3), ("d", 1, 1, 1), ("ts", 1), ("re", 1, 1),
    ("d", 1, 2, 3), ("re", 1, 2), ("d", 1, 0, 0), ("d", 1, 2, 0), ("mix", 0), ("d", 1, 1, 0), ("mix", 1), ("tf", 2),
    ("tf", 4), ("mf", 0), ("tf", 3), ("tf", 1), ("mix", 2), ("mf", 1), ("m", 0), ("dr", 2, 0), ("d", 2, 0, 2),
    ("d", 2, 0, 3), ("d", 2, 0, 1), ("mf", 2), ("ts", 0), ("m", 1), ("dr", 2, 1), ("d", 2, 1, 2), ("re", 2, 0),
    ("d", 2, 1, 1), ("d", 2, 1, 3), ("m", 2), ("dr", 2, 2), ("d", 2, 2, 2), ("tf", 0), ("d", 2, 2, 3),
    ("d", 2, 2, 1), ("re", 2, 1), ("re", 2, 2), ("d", 2, 0, 0), ("d", 2, 1, 0), ("fin", 0), ("d", 2, 2, 0),
    ("fin", 1), ("fin", 2), ("col", 0), ("col", 1), ("col", 2),
)


def kernel(
    count, w_hbm, t_hbm, v_hbm, out,
    w_in, t_in, v_in, load_sem, live,
    w_t, t_t, v_t,
    ts, tl, tl_s1, tl_r1, tl_s2, tl_r2, tl_sw,
    ws, wp, w_sw,
    vp, vm, vr, vx, v_as, v_ar, v_s1, v_r1, v_s2, v_r2,
    tp, tm, tr, tx, t_as, t_ar, t_s1, t_r1, t_s2, t_r2,
    mb, m_s1, m_r1, m_s2, m_r2,
    lhs1, cs1, own1, d1, d2, d_s1, d_r1, d_s2, d_r2,
    lhs2, cs2, own2, e1, e2, e_s1, e_r1, e_s2, e_r2,
    fo, ob, o_t, o_s, o_r,
):
    row, col = lax.axis_index("row"), lax.axis_index("col")
    y, c = row // 2, lax.rem(row, 2)
    z, x = col // 4, lax.rem(col, 4)
    a, b = jnp.where(c == 0, z, x), jnp.where(c == 0, x, z)

    def at(i, n):
        return lax.rem(i + n + 8, 4)

    def dev(dx=0, dy=0, dz=0, core=None):
        return (at(y, dy) * 2 + (c if core is None else core), at(z, dz) * 4 + at(x, dx))

    def ring(n):
        return (row, jnp.where(c == 0, at(z, n) * 4 + x, z * 4 + at(x, n)))

    def line(n):
        return (row, jnp.where(c == 0, z * 4 + at(x, n), at(z, n) * 4 + x))

    partner = dev(core=1 - c)
    pending = []

    def remote(src, dst, ss, rs, to):
        return pltpu.make_async_remote_copy(src, dst, ss, rs, device_id=to, device_id_type=MESH)

    def send(src, dst, ss, rs, to):
        copy = remote(src, dst, ss, rs, to)
        copy.start()
        pending.append(copy)

    def got(dst, rs):
        remote(dst, dst, rs, rs, partner).wait_recv()

    loads = [
        pltpu.make_async_copy(s, d, load_sem.at[i])
        for i, (s, d) in enumerate(((v_hbm, v_in), (t_hbm, t_in), (w_hbm, w_in)))
    ]
    for load in loads:
        load.start()
    barrier = pltpu.get_barrier_semaphore()
    friends = [partner] + [dev(dx=n, core=k) for n in (1, 2, 3) for k in (0, 1)]
    friends += [dev(dz=n, core=k) for n in (1, -1) for k in (0, 1)] + [dev(dy=n) for n in (1, -1)]
    for friend in friends:
        pl.semaphore_signal(barrier, inc=1, device_id=friend, device_id_type=MESH)
    for n in range(4):
        core = y // 2

        @pl.when((c == 1) & jnp.logical_not((n == z) & (y == z) & (core == 1)))
        def _():
            source = (z * 2 + core, n * 4 + x)
            pl.semaphore_signal(barrier, inc=1, device_id=source, device_id_type=MESH)

    greetings = len(friends) + 2 - jnp.where((c == 1) & (y == z) & (y >= 2), 1, 0)
    for h in range(2):
        cid = col * COLS + lax.broadcasted_iota(jnp.int32, (COLS, ROWS), 0)
        rid = row * ROWS + lax.broadcasted_iota(jnp.int32, (COLS, ROWS), 1)
        live[h] = jnp.where((rid < count[h]) & (cid < count[h]), 1.0, 0.0).astype(BF16)

    def turn(src, dst, h):
        dst[h] = jnp.transpose(src[h] * live[h])

    def pack_rows(ref, dst, h, q):
        r0 = q * R
        dst[h, q, 0:R] = ref[h, r0 : r0 + R, 0:128]
        dst[h, q, R : 2 * R] = ref[h, r0 : r0 + R, 128:256]
        strips = [ref[h, r0 + g * G : r0 + g * G + G, 256:288].astype(F32) for g in range(4)]
        dst[h, q, 2 * R : PR] = jnp.concatenate(strips, axis=1).astype(BF16)

    def pack_right(ref, dst, h, s):
        r0 = s * H
        dst[h, s, 0:H] = ref[h, r0 : r0 + H, 0:128]
        dst[h, s, H : 2 * H] = ref[h, r0 : r0 + H, 128:256]
        strips = []
        for g in range(4):
            n = min(RG, H - g * RG)
            strip = ref[h, r0 + g * RG : r0 + g * RG + n, 256:288].astype(F32)
            if n < RG:
                strip = jnp.concatenate([strip, jnp.zeros((RG - n, 32), F32)], axis=0)
            strips.append(strip)
        dst[h, s, 2 * H : PV] = jnp.concatenate(strips, axis=1).astype(BF16)

    def either(mine, copies, to, go):
        @pl.when(jnp.logical_not(mine))
        def _():
            for copy in copies:
                if go:
                    remote(*copy, to).start()
                else:
                    remote(*copy, to).wait_send()

        if go:

            @pl.when(mine)
            def _():
                for src, dst, _, rs in copies:
                    pltpu.make_async_copy(src, dst, rs).start()

    def exchange(ops, h, go):
        for s in range(2):
            to = 2 * c + s
            k, n = (y, x) if h == 0 else (to, z)
            copies = (
                (ops.p.at[h, s, 0 : 2 * H], ops.m.at[k, n], ops.as_.at[s, h, 0], ops.ar.at[n, 0]),
                (ops.p.at[h, s, 2 * H : PV], ops.x.at[n], ops.as_.at[s, h, 1], ops.ar.at[n, 1]),
            )
            if h == 0:
                either((to == x) & (c == 0), copies, (y * 2, z * 4 + to), go)
            else:
                either((to == y) & (y == z) & (c == 1), copies, (to * 2 + 1, y * 4 + x), go)

    def y_send(ops, o):
        if o < 4:
            src = ops.m.at[y, at(b, o)]
            got(src, ops.ar.at[at(b, o), 0])
        else:
            for i in range(4):
                got(ops.x.at[i], ops.ar.at[i, 1])
            for g, v in enumerate(swap4([ops.x[i].astype(F32) for i in range(4)])):
                n = min(RG, H - g * RG)
                ops.r[y, g * RG : g * RG + n] = v[:n].astype(BF16)
            src = ops.r.at[y]
        for d in (0, 1):
            send(src, src, ops.s1.at[d, o], ops.r1.at[d, o], dev(dy=1 - 2 * d))

    def y_part(ops, k, o, d):
        if o < 4:
            return ops.m.at[k, at(b, o), pl.ds(d * H, H)]
        return ops.r.at[k, pl.ds(d * (H // 2), H // 2)]

    def y_forward(ops, o):
        for d in (0, 1):
            k = at(y, 2 * d - 1)
            got(ops.m.at[k, at(b, o)] if o < 4 else ops.r.at[k], ops.r1.at[d, o])
            part = y_part(ops, k, o, d)
            send(part, part, ops.s2.at[d, o], ops.r2.at[d, o], dev(dy=1 - 2 * d))

    def y_last(ops, o):
        for d in (0, 1):
            got(y_part(ops, at(y, 2), o, d), ops.r2.at[d, o])

    def ring_forward(buf, r1, s2, r2, q):
        for d in (0, 1):
            k, p = at(a, 2 * d - 1), d * Q + q
            got(buf.at[k, p], r1.at[d, p])
            send(buf.at[k, p], buf.at[k, p], s2.at[d, q], r2.at[d, q], ring(1 - 2 * d))

    def ring_last(buf, r1, r2, q):
        for d in (0, 1):
            k, p = at(a, 2 * d - 1), (1 - d) * Q + q
            got(buf.at[k, p], r1.at[d, p])
            got(buf.at[at(a, 2), d * Q + q], r2.at[d, q])

    def make_left(buf, lhs, q):
        for half in (0, 1):
            p, r0 = half * Q + q, half * R
            for k in range(4):
                lhs[q, r0 : r0 + R, k * 256 : k * 256 + 128] = buf[k, p, 0:R]
                lhs[q, r0 : r0 + R, k * 256 + 128 : k * 256 + 256] = buf[k, p, R : 2 * R]
            for g, v in enumerate(swap4([buf[k, p, 2 * R : PR].astype(F32) for k in range(4)])):
                lhs[q, r0 + g * G : r0 + g * G + G, 1024:1152] = v.astype(BF16)

    def dot_rest(st, q):
        vr = st.ops.r
        y_last(st.ops, 4) if q == 0 else None
        right = jnp.concatenate([vr[k, 0:256] for k in range(4)] + [vr[k, 256:H] for k in range(4)], axis=0)
        part = jnp.dot(st.lhs[q], right, preferred_element_type=F32)
        for half in (0, 1):
            p = half * Q + q
            by = swap4([part[half * R + g * G : half * R + g * G + G] for g in range(4)])
            for o in range(4):
                t = at(b, o)
                v = jnp.where(t == 0, by[0], jnp.where(t == 1, by[1], jnp.where(t == 2, by[2], by[3])))
                if o == 0:
                    st.own[p, 2 * R : PR] = v
                else:
                    st.cs[o - 1, p, 2 * R : PR] = v.astype(BF16)

    def dot_main(st, q, o):
        vm, t = st.ops.m, at(b, o)
        y_last(st.ops, o) if q == 0 else None
        big = [jnp.concatenate([vm[k, t, 0:256], vm[k, t, H : H + 256]], axis=1) for k in range(4)]
        small = [jnp.concatenate([vm[k, t, 256:H], vm[k, t, H + 256 : 2 * H]], axis=1) for k in range(4)]
        part = jnp.dot(st.lhs[q], jnp.concatenate(big + small, axis=0), preferred_element_type=F32)
        for half in (0, 1):
            p = half * Q + q
            for lane in (0, 1):
                v = part[half * R : half * R + R, lane * 128 : lane * 128 + 128]
                if o == 0:
                    st.own[p, lane * R : lane * R + R] = v
                else:
                    st.cs[o - 1, p, lane * R : lane * R + R] = v.astype(BF16)
        if o == 2:
            for d in (0, 1):
                send(st.cs.at[1, d * Q + q], st.l1.at[d, q], st.s1.at[d, q], st.r1.at[d, q], line(1 - 2 * d))
        elif o:
            d = o // 2
            p = (1 - d) * Q + q
            send(st.cs.at[2 * d, p], st.l2.at[d, p], st.s2.at[d, p], st.r2.at[d, p], line(1 - 2 * d))

    def relay(st, q):
        for d in (0, 1):
            p = d * Q + q
            got(st.l1.at[d, q], st.r1.at[d, q])
            st.cs[2 * d, p] = (st.cs[2 * d, p].astype(F32) + st.l1[d, q].astype(F32)).astype(BF16)
            send(st.cs.at[2 * d, p], st.l2.at[d, p], st.s2.at[d, p], st.r2.at[d, p], line(1 - 2 * d))

    def total(st, p):
        for d in (0, 1):
            got(st.l2.at[d, p], st.r2.at[d, p])
        return st.own[p] + st.l2[0, p].astype(F32) + st.l2[1, p].astype(F32)

    def unpack(v, h, q):
        r0 = q * R
        o_t[h, r0 : r0 + R, 0:128] = v[0:R].astype(BF16)
        o_t[h, r0 : r0 + R, 128:256] = v[R : 2 * R].astype(BF16)
        for g in range(4):
            strip = v[2 * R : PR]
            if g:
                strip = pltpu.roll(strip, 128 - 32 * g, 1)
            o_t[h, r0 + g * G : r0 + g * G + G, 256:288] = strip[:, 0:32].astype(BF16)

    def turn_back(h, q):
        if q == 1:
            out[h, :, 0:384] = jnp.transpose(o_t[h, 0:384])
        if q == 2:
            out[h, :, 384:576] = jnp.transpose(o_t[h, 384:576])

    v_ops = Ops(vp, vm, vr, vx, v_as, v_ar, v_s1, v_r1, v_s2, v_r2)
    t_ops = Ops(tp, tm, tr, tx, t_as, t_ar, t_s1, t_r1, t_s2, t_r2)
    stages = {
        1: Stage(v_ops, lhs1, cs1, own1, d1, d2, d_s1, d_r1, d_s2, d_r2),
        2: Stage(t_ops, lhs2, cs2, own2, e1, e2, e_s1, e_r1, e_s2, e_r2),
    }

    def step_p(h):
        if h == 1:
            loads[0].wait()
        turn(v_in, v_t, h)
        for s in range(2):
            pack_right(v_t, vp, h, s)

    def step_b():
        pl.semaphore_wait(barrier, greetings)

    def step_v(h):
        exchange(v_ops, h, True)

    def step_pt():
        loads[1].wait()
        for h in range(2):
            turn(t_in, t_t, h)
            for q in range(Q):
                pack_rows(t_t, ts, h, q)
        for q in range(Q):
            tl[a, c * Q + q] = ts[c, q]

    def step_t(q):
        for h in range(2):
            for d in (0, 1):
                to = dev(dz=1 - 2 * d, core=0) if h == 0 else dev(dx=1 - 2 * d, core=1)
                place = z if h == 0 else x
                send(ts.at[h, q], tl.at[place, c * Q + q], tl_s1.at[d, h, q], tl_r1.at[d, c * Q + q], to)
        send(ts.at[1 - c, q], tl.at[b, c * Q + q], tl_sw.at[0, q], tl_sw.at[1, q], partner)

    def step_r(h):
        for s in range(2):
            pack_right(t_t, tp, h, s)
        exchange(t_ops, h, True)

    def step_w():
        loads[2].wait()
        for h in range(2):
            turn(w_in, w_t, h)
            for q in range(Q):
                pack_rows(w_t, ws, h, q)
        send(ws.at[1 - c], wp.at[pl.ds(c * Q, Q)], w_sw.at[0], w_sw.at[1], partner)
        for q in range(Q):
            wp[c * Q + q] = ws[c, q]

    def step_left(q):
        ring_last(tl, tl_r1, tl_r2, q)
        got(tl.at[a, (1 - c) * Q + q], tl_sw.at[1, q])
        make_left(tl, lhs1, q)

    def step_mix(q):
        if q == 0:
            got(wp.at[pl.ds((1 - c) * Q, Q)], w_sw.at[1])
        for half in (0, 1):
            p = half * Q + q
            mb[a, p] = (wp[p].astype(F32) + 0.5 * total(stages[1], p)).astype(BF16)
            for d in (0, 1):
                send(mb.at[a, p], mb.at[a, p], m_s1.at[d, p], m_r1.at[d, p], ring(1 - 2 * d))

    def step_mixed(q):
        ring_last(mb, m_r1, m_r2, q)
        make_left(mb, lhs2, q)

    def step_finish(q):
        for half in (0, 1):
            fo[half, q] = total(stages[2], half * Q + q).astype(BF16)
        send(fo.at[1 - c, q], ob.at[q], o_s.at[q], o_r.at[q], partner)
        unpack(fo[c, q].astype(F32), c, q)
        turn_back(c, q)

    def step_collect(q):
        got(ob.at[q], o_r.at[q])
        unpack(ob[q].astype(F32), 1 - c, q)
        turn_back(1 - c, q)

    steps = {
        "v": step_v, "t": step_t, "r": step_r, "w": step_w,
        "p": step_p, "b": step_b, "pt": step_pt,
        "vs": lambda o: y_send(v_ops, o), "vf": lambda o: y_forward(v_ops, o),
        "ts": lambda o: y_send(t_ops, o), "tf": lambda o: y_forward(t_ops, o),
        "lf": lambda q: ring_forward(tl, tl_r1, tl_s2, tl_r2, q), "l": step_left,
        "mf": lambda q: ring_forward(mb, m_r1, m_s2, m_r2, q), "m": step_mixed,
        "dr": lambda s, q: dot_rest(stages[s], q), "d": lambda s, q, o: dot_main(stages[s], q, o),
        "re": lambda s, q: relay(stages[s], q), "mix": step_mix,
        "fin": step_finish, "col": step_collect,
    }
    for step in SCHEDULE:
        steps[step[0]](*step[1:])
    for ops in (v_ops, t_ops):
        for h in (0, 1):
            exchange(ops, h, False)
    for copy in pending:
        copy.wait_send()


class Ops(NamedTuple):
    p: Any
    m: Any
    r: Any
    x: Any
    as_: Any
    ar: Any
    s1: Any
    r1: Any
    s2: Any
    r2: Any


class Stage(NamedTuple):
    ops: Any
    lhs: Any
    cs: Any
    own: Any
    l1: Any
    l2: Any
    s1: Any
    r1: Any
    s2: Any
    r2: Any


def per_device(pair_count, coupling, amplitudes, integrals):
    dma = pltpu.SemaphoreType.DMA
    coupling, amplitudes, integrals = (jnp.transpose(v, (0, 2, 1)) for v in (coupling, amplitudes, integrals))
    turned, shard = (2, COLS, ROWS), (2, ROWS, COLS)

    def piece(*lead, dtype=BF16):
        return pltpu.VMEM((*lead, PR, 128), dtype)

    def right():
        return [
            pltpu.VMEM((2, 2, PV, 128), BF16), pltpu.VMEM((4, 4, 2 * H, 128), BF16), pltpu.VMEM((4, H, 128), BF16),
            pltpu.VMEM((4, RG, 128), BF16), dma((2, 2, 2)), dma((4, 2)),
            dma((2, 5)), dma((2, 5)), dma((2, 5)), dma((2, 5)),
        ]

    def sums():
        return [
            pltpu.VMEM((Q, 2 * R, 1152), BF16), piece(3, 2 * Q), piece(2 * Q, dtype=F32), piece(2, Q), piece(2, 2 * Q),
            dma((2, Q)), dma((2, Q)), dma((2, 2 * Q)), dma((2, 2 * Q)),
        ]

    scratch = [pltpu.VMEM(turned, BF16)] * 3 + [dma((3,)), pltpu.VMEM(turned, BF16)] + [pltpu.VMEM(shard, BF16)] * 3
    scratch += [piece(2, Q), piece(4, 2 * Q), dma((2, 2, Q)), dma((2, 2 * Q)), dma((2, Q)), dma((2, Q)), dma((2, Q))]
    scratch += [piece(2, Q), piece(2 * Q), dma((2,))]
    scratch += right() + right()
    scratch += [piece(4, 2 * Q), dma((2, 2 * Q)), dma((2, 2 * Q)), dma((2, Q)), dma((2, Q))]
    scratch += sums() + sums()
    scratch += [piece(2, Q), piece(Q), pltpu.VMEM(shard, BF16), dma((Q,)), dma((Q,))]
    result = pl.pallas_call(
        kernel,
        out_shape=jax.ShapeDtypeStruct(turned, BF16),
        in_specs=[pl.BlockSpec(memory_space=pltpu.SMEM)] + [pl.BlockSpec(memory_space=pl.ANY)] * 3,
        out_specs=pl.BlockSpec(memory_space=pltpu.VMEM),
        scratch_shapes=scratch,
        compiler_params=pltpu.CompilerParams(collective_id=0, has_side_effects=True, vmem_limit_bytes=56 << 20),
        cost_estimate=pl.CostEstimate(flops=6115295232, bytes_accessed=2654208, transcendentals=0),
        name="cycle",
    )(pair_count, coupling, amplitudes, integrals)
    return jnp.transpose(result, (0, 2, 1))


def solution(mesh):
    split = P(None, "row", "col")
    return jax.shard_map(per_device, mesh=mesh, in_specs=(P(), split, split, split), out_specs=split, check_vma=False)
```

```python
from typing import Any, NamedTuple

import jax
import jax.numpy as jnp
from jax import lax
from jax.experimental import pallas as pl
from jax.experimental.pallas import tpu as pltpu
from jax.sharding import PartitionSpec as P

MESH = pl.DeviceIdType.MESH
F32, BF16 = jnp.float32, jnp.bfloat16
ROWS, COLS = 576, 288
PIECES = (192, 192, 192)
Q = len(PIECES)
START = tuple(sum(PIECES[:q]) for q in range(Q))
RMAX = max(PIECES)
PMAX = 2 * RMAX + RMAX // 4
H = ROWS // 2
RG = 80
PV = 2 * H + RG


def sizes(q):
    r = PIECES[q]
    return r, r // 4, 2 * r + r // 4


def swap4(parts):
    group = lax.broadcasted_iota(jnp.int32, parts[0].shape, 1) // 32
    out = []
    for b in range(4):
        total = None
        for a in range(4):
            v = parts[a] if a == b else pltpu.roll(parts[a], (32 * (a - b)) % 128, 1)
            total = v if total is None else jnp.where(group == a, v, total)
        out.append(total)
    return out

SCHEDULE = (
    ("p", 1), ("b",), ("v", 1), ("p", 0), ("pt",), ("v", 0), ("r", 1), ("r", 0), ("vs", 2), ("t", 0), ("vs", 1),
    ("vs", 4), ("vs", 3), ("t", 1), ("t", 2), ("lf", 0), ("lf", 2), ("vf", 4), ("w",), ("lf", 1), ("vf", 2),
    ("vf", 1), ("l", 0), ("vf", 3), ("vs", 0), ("l", 2), ("dr", 1, 0), ("dr", 1, 2), ("l", 1), ("d", 1, 0, 2),
    ("d", 1, 2, 2), ("dr", 1, 1), ("d", 1, 1, 2), ("ts", 2), ("d", 1, 0, 1), ("d", 1, 0, 3), ("d", 1, 1, 3),
    ("d", 1, 2, 1), ("vf", 0), ("re", 1, 0), ("ts", 4), ("d", 1, 1, 1), ("ts", 3), ("d", 1, 2, 3), ("ts", 1),
    ("re", 1, 1), ("d", 1, 0, 0), ("re", 1, 2), ("mix", 0), ("d", 1, 2, 0), ("d", 1, 1, 0), ("tf", 2), ("mix", 1),
    ("tf", 4), ("mf", 0), ("tf", 3), ("tf", 1), ("mix", 2), ("mf", 1), ("m", 0), ("dr", 2, 0), ("d", 2, 0, 2),
    ("d", 2, 0, 3), ("d", 2, 0, 1), ("mf", 2), ("ts", 0), ("m", 1), ("dr", 2, 1), ("d", 2, 1, 2), ("re", 2, 0),
    ("d", 2, 1, 1), ("d", 2, 1, 3), ("m", 2), ("dr", 2, 2), ("d", 2, 2, 2), ("tf", 0), ("d", 2, 2, 3),
    ("d", 2, 2, 1), ("re", 2, 1), ("re", 2, 2), ("d", 2, 0, 0), ("d", 2, 1, 0), ("fin", 0), ("d", 2, 2, 0),
    ("fin", 1), ("fin", 2), ("col", 0), ("col", 1), ("col", 2),
)


def kernel(
    count, w_hbm, t_hbm, v_hbm, out,
    w_in, t_in, v_in, load_sem, live,
    w_t, t_t, v_t,
    ts, tl, tl_s1, tl_r1, tl_s2, tl_r2, tl_sw,
    ws, wp, w_sw,
    vp, vm, vr, vx, v_as, v_ar, v_s1, v_r1, v_s2, v_r2,
    tp, tm, tr, tx, t_as, t_ar, t_s1, t_r1, t_s2, t_r2,
    mb, m_s1, m_r1, m_s2, m_r2,
    lhs1, cs1, own1, d1, d2, d_s1, d_r1, d_s2, d_r2,
    lhs2, cs2, own2, e1, e2, e_s1, e_r1, e_s2, e_r2,
    fo, ob, o_t, o_s, o_r,
):
    row, col = lax.axis_index("row"), lax.axis_index("col")
    y, c = row // 2, lax.rem(row, 2)
    z, x = col // 4, lax.rem(col, 4)
    a, b = jnp.where(c == 0, z, x), jnp.where(c == 0, x, z)

    def at(i, n):
        return lax.rem(i + n + 8, 4)

    def dev(dx=0, dy=0, dz=0, core=None):
        return (at(y, dy) * 2 + (c if core is None else core), at(z, dz) * 4 + at(x, dx))

    def ring(n):
        return (row, jnp.where(c == 0, at(z, n) * 4 + x, z * 4 + at(x, n)))

    def line(n):
        return (row, jnp.where(c == 0, z * 4 + at(x, n), at(z, n) * 4 + x))

    partner = dev(core=1 - c)
    pending = []

    def remote(src, dst, ss, rs, to):
        return pltpu.make_async_remote_copy(src, dst, ss, rs, device_id=to, device_id_type=MESH)

    def send(src, dst, ss, rs, to):
        copy = remote(src, dst, ss, rs, to)
        copy.start()
        pending.append(copy)

    def got(dst, rs):
        remote(dst, dst, rs, rs, partner).wait_recv()

    loads = [
        pltpu.make_async_copy(s, d, load_sem.at[i])
        for i, (s, d) in enumerate(((v_hbm, v_in), (t_hbm, t_in), (w_hbm, w_in)))
    ]
    for load in loads:
        load.start()
    barrier = pltpu.get_barrier_semaphore()
    friends = [partner] + [dev(dx=n, core=k) for n in (1, 2, 3) for k in (0, 1)]
    friends += [dev(dz=n, core=k) for n in (1, -1) for k in (0, 1)] + [dev(dy=n) for n in (1, -1)]
    for friend in friends:
        pl.semaphore_signal(barrier, inc=1, device_id=friend, device_id_type=MESH)
    for n in range(4):
        core = y // 2

        @pl.when((c == 1) & jnp.logical_not((n == z) & (y == z) & (core == 1)))
        def _():
            source = (z * 2 + core, n * 4 + x)
            pl.semaphore_signal(barrier, inc=1, device_id=source, device_id_type=MESH)

    greetings = len(friends) + 2 - jnp.where((c == 1) & (y == z) & (y >= 2), 1, 0)
    for h in range(2):
        cid = col * COLS + lax.broadcasted_iota(jnp.int32, (COLS, ROWS), 0)
        rid = row * ROWS + lax.broadcasted_iota(jnp.int32, (COLS, ROWS), 1)
        live[h] = jnp.where((rid < count[h]) & (cid < count[h]), 1.0, 0.0).astype(BF16)

    def turn(src, dst, h):
        dst[h] = jnp.transpose(src[h] * live[h])

    def pack_rows(ref, dst, h, q):
        R, G, PR = sizes(q)
        r0 = START[q]
        dst[h, q, 0:R] = ref[h, r0 : r0 + R, 0:128]
        dst[h, q, R : 2 * R] = ref[h, r0 : r0 + R, 128:256]
        strips = [ref[h, r0 + g * G : r0 + g * G + G, 256:288].astype(F32) for g in range(4)]
        dst[h, q, 2 * R : PR] = jnp.concatenate(strips, axis=1).astype(BF16)

    def pack_right(ref, dst, h, s):
        r0 = s * H
        dst[h, s, 0:H] = ref[h, r0 : r0 + H, 0:128]
        dst[h, s, H : 2 * H] = ref[h, r0 : r0 + H, 128:256]
        strips = []
        for g in range(4):
            n = min(RG, H - g * RG)
            strip = ref[h, r0 + g * RG : r0 + g * RG + n, 256:288].astype(F32)
            if n < RG:
                strip = jnp.concatenate([strip, jnp.zeros((RG - n, 32), F32)], axis=0)
            strips.append(strip)
        dst[h, s, 2 * H : PV] = jnp.concatenate(strips, axis=1).astype(BF16)

    def either(mine, copies, to, go):
        @pl.when(jnp.logical_not(mine))
        def _():
            for copy in copies:
                if go:
                    remote(*copy, to).start()
                else:
                    remote(*copy, to).wait_send()

        if go:

            @pl.when(mine)
            def _():
                for src, dst, _, rs in copies:
                    pltpu.make_async_copy(src, dst, rs).start()

    def exchange(ops, h, go):
        for s in range(2):
            to = 2 * c + s
            k, n = (y, x) if h == 0 else (to, z)
            copies = (
                (ops.p.at[h, s, 0 : 2 * H], ops.m.at[k, n], ops.as_.at[s, h, 0], ops.ar.at[n, 0]),
                (ops.p.at[h, s, 2 * H : PV], ops.x.at[n], ops.as_.at[s, h, 1], ops.ar.at[n, 1]),
            )
            if h == 0:
                either((to == x) & (c == 0), copies, (y * 2, z * 4 + to), go)
            else:
                either((to == y) & (y == z) & (c == 1), copies, (to * 2 + 1, y * 4 + x), go)

    def y_send(ops, o):
        if o < 4:
            src = ops.m.at[y, at(b, o)]
            got(src, ops.ar.at[at(b, o), 0])
        else:
            for i in range(4):
                got(ops.x.at[i], ops.ar.at[i, 1])
            for g, v in enumerate(swap4([ops.x[i].astype(F32) for i in range(4)])):
                n = min(RG, H - g * RG)
                ops.r[y, g * RG : g * RG + n] = v[:n].astype(BF16)
            src = ops.r.at[y]
        for d in (0, 1):
            send(src, src, ops.s1.at[d, o], ops.r1.at[d, o], dev(dy=1 - 2 * d))

    def y_part(ops, k, o, d):
        if o < 4:
            return ops.m.at[k, at(b, o), pl.ds(d * H, H)]
        return ops.r.at[k, pl.ds(d * (H // 2), H // 2)]

    def y_forward(ops, o):
        for d in (0, 1):
            k = at(y, 2 * d - 1)
            got(ops.m.at[k, at(b, o)] if o < 4 else ops.r.at[k], ops.r1.at[d, o])
            part = y_part(ops, k, o, d)
            send(part, part, ops.s2.at[d, o], ops.r2.at[d, o], dev(dy=1 - 2 * d))

    def y_last(ops, o):
        for d in (0, 1):
            got(y_part(ops, at(y, 2), o, d), ops.r2.at[d, o])

    def ring_forward(buf, r1, s2, r2, q):
        for d in (0, 1):
            k, p = at(a, 2 * d - 1), d * Q + q
            part = buf.at[k, p, 0 : sizes(q)[2]]
            got(part, r1.at[d, p])
            send(part, part, s2.at[d, q], r2.at[d, q], ring(1 - 2 * d))

    def ring_last(buf, r1, r2, q):
        n = sizes(q)[2]
        for d in (0, 1):
            k, p = at(a, 2 * d - 1), (1 - d) * Q + q
            got(buf.at[k, p, 0:n], r1.at[d, p])
            got(buf.at[at(a, 2), d * Q + q, 0:n], r2.at[d, q])

    def make_left(buf, lhs, q):
        R, G, PR = sizes(q)
        for half in (0, 1):
            p, r0 = half * Q + q, half * R
            for k in range(4):
                lhs[q, r0 : r0 + R, k * 256 : k * 256 + 128] = buf[k, p, 0:R]
                lhs[q, r0 : r0 + R, k * 256 + 128 : k * 256 + 256] = buf[k, p, R : 2 * R]
            for g, v in enumerate(swap4([buf[k, p, 2 * R : PR].astype(F32) for k in range(4)])):
                lhs[q, r0 + g * G : r0 + g * G + G, 1024:1152] = v.astype(BF16)

    def dot_rest(st, q):
        R, G, PR = sizes(q)
        vr = st.ops.r
        y_last(st.ops, 4) if q == 0 else None
        right = jnp.concatenate([vr[k, 0:256] for k in range(4)] + [vr[k, 256:H] for k in range(4)], axis=0)
        part = jnp.dot(st.lhs[q, 0 : 2 * R], right, preferred_element_type=F32)
        for half in (0, 1):
            p = half * Q + q
            by = swap4([part[half * R + g * G : half * R + g * G + G] for g in range(4)])
            for o in range(4):
                t = at(b, o)
                v = jnp.where(t == 0, by[0], jnp.where(t == 1, by[1], jnp.where(t == 2, by[2], by[3])))
                if o == 0:
                    st.own[p, 2 * R : PR] = v
                else:
                    st.cs[o - 1, p, 2 * R : PR] = v.astype(BF16)

    def dot_main(st, q, o):
        R, _, PR = sizes(q)
        vm, t = st.ops.m, at(b, o)
        y_last(st.ops, o) if q == 0 else None
        big = [jnp.concatenate([vm[k, t, 0:256], vm[k, t, H : H + 256]], axis=1) for k in range(4)]
        small = [jnp.concatenate([vm[k, t, 256:H], vm[k, t, H + 256 : 2 * H]], axis=1) for k in range(4)]
        part = jnp.dot(st.lhs[q, 0 : 2 * R], jnp.concatenate(big + small, axis=0), preferred_element_type=F32)
        for half in (0, 1):
            p = half * Q + q
            for lane in (0, 1):
                v = part[half * R : half * R + R, lane * 128 : lane * 128 + 128]
                if o == 0:
                    st.own[p, lane * R : lane * R + R] = v
                else:
                    st.cs[o - 1, p, lane * R : lane * R + R] = v.astype(BF16)
        if o == 2:
            for d in (0, 1):
                send(st.cs.at[1, d * Q + q, 0:PR], st.l1.at[d, q, 0:PR], st.s1.at[d, q], st.r1.at[d, q], line(1 - 2 * d))
        elif o:
            d = o // 2
            p = (1 - d) * Q + q
            send(st.cs.at[2 * d, p, 0:PR], st.l2.at[d, p, 0:PR], st.s2.at[d, p], st.r2.at[d, p], line(1 - 2 * d))

    def relay(st, q):
        PR = sizes(q)[2]
        for d in (0, 1):
            p = d * Q + q
            got(st.l1.at[d, q, 0:PR], st.r1.at[d, q])
            st.cs[2 * d, p, 0:PR] = (st.cs[2 * d, p, 0:PR].astype(F32) + st.l1[d, q, 0:PR].astype(F32)).astype(BF16)
            send(st.cs.at[2 * d, p, 0:PR], st.l2.at[d, p, 0:PR], st.s2.at[d, p], st.r2.at[d, p], line(1 - 2 * d))

    def total(st, half, q):
        p, n = half * Q + q, sizes(q)[2]
        for d in (0, 1):
            got(st.l2.at[d, p, 0:n], st.r2.at[d, p])
        return st.own[p, 0:n] + st.l2[0, p, 0:n].astype(F32) + st.l2[1, p, 0:n].astype(F32)

    def unpack(v, h, q):
        R, G, PR = sizes(q)
        r0 = START[q]
        o_t[h, r0 : r0 + R, 0:128] = v[0:R].astype(BF16)
        o_t[h, r0 : r0 + R, 128:256] = v[R : 2 * R].astype(BF16)
        for g in range(4):
            strip = v[2 * R : PR]
            if g:
                strip = pltpu.roll(strip, 128 - 32 * g, 1)
            o_t[h, r0 + g * G : r0 + g * G + G, 256:288] = strip[:, 0:32].astype(BF16)

    def turn_back(h, q):
        if q == Q - 2:
            out[h, :, 0 : START[Q - 1]] = jnp.transpose(o_t[h, 0 : START[Q - 1]])
        if q == Q - 1:
            out[h, :, START[Q - 1] : ROWS] = jnp.transpose(o_t[h, START[Q - 1] : ROWS])

    v_ops = Ops(vp, vm, vr, vx, v_as, v_ar, v_s1, v_r1, v_s2, v_r2)
    t_ops = Ops(tp, tm, tr, tx, t_as, t_ar, t_s1, t_r1, t_s2, t_r2)
    stages = {
        1: Stage(v_ops, lhs1, cs1, own1, d1, d2, d_s1, d_r1, d_s2, d_r2),
        2: Stage(t_ops, lhs2, cs2, own2, e1, e2, e_s1, e_r1, e_s2, e_r2),
    }

    def step_p(h):
        if h == 1:
            loads[0].wait()
        turn(v_in, v_t, h)
        for s in range(2):
            pack_right(v_t, vp, h, s)

    def step_b():
        pl.semaphore_wait(barrier, greetings)

    def step_v(h):
        exchange(v_ops, h, True)

    def step_pt():
        loads[1].wait()
        for h in range(2):
            turn(t_in, t_t, h)
            for q in range(Q):
                pack_rows(t_t, ts, h, q)
        for q in range(Q):
            n = sizes(q)[2]
            tl[a, c * Q + q, 0:n] = ts[c, q, 0:n]

    def step_t(q):
        n = sizes(q)[2]
        for h in range(2):
            for d in (0, 1):
                to = dev(dz=1 - 2 * d, core=0) if h == 0 else dev(dx=1 - 2 * d, core=1)
                dst = tl.at[z if h == 0 else x, c * Q + q, 0:n]
                send(ts.at[h, q, 0:n], dst, tl_s1.at[d, h, q], tl_r1.at[d, c * Q + q], to)
        send(ts.at[1 - c, q, 0:n], tl.at[b, c * Q + q, 0:n], tl_sw.at[0, q], tl_sw.at[1, q], partner)

    def step_r(h):
        for s in range(2):
            pack_right(t_t, tp, h, s)
        exchange(t_ops, h, True)

    def step_w():
        loads[2].wait()
        for h in range(2):
            turn(w_in, w_t, h)
            for q in range(Q):
                pack_rows(w_t, ws, h, q)
        for q in range(Q):
            n = sizes(q)[2]
            send(ws.at[1 - c, q, 0:n], wp.at[c * Q + q, 0:n], w_sw.at[0, q], w_sw.at[1, q], partner)
            wp[c * Q + q, 0:n] = ws[c, q, 0:n]

    def step_left(q):
        ring_last(tl, tl_r1, tl_r2, q)
        got(tl.at[a, (1 - c) * Q + q, 0 : sizes(q)[2]], tl_sw.at[1, q])
        make_left(tl, lhs1, q)

    def step_mix(q):
        n = sizes(q)[2]
        got(wp.at[(1 - c) * Q + q, 0:n], w_sw.at[1, q])
        for half in (0, 1):
            p = half * Q + q
            mb[a, p, 0:n] = (wp[p, 0:n].astype(F32) + 0.5 * total(stages[1], half, q)).astype(BF16)
            part = mb.at[a, p, 0:n]
            for d in (0, 1):
                send(part, part, m_s1.at[d, p], m_r1.at[d, p], ring(1 - 2 * d))

    def step_mixed(q):
        ring_last(mb, m_r1, m_r2, q)
        make_left(mb, lhs2, q)

    def step_finish(q):
        n = sizes(q)[2]
        for half in (0, 1):
            fo[half, q, 0:n] = total(stages[2], half, q).astype(BF16)
        send(fo.at[1 - c, q, 0:n], ob.at[q, 0:n], o_s.at[q], o_r.at[q], partner)
        unpack(fo[c, q, 0:n].astype(F32), c, q)
        turn_back(c, q)

    def step_collect(q):
        n = sizes(q)[2]
        got(ob.at[q, 0:n], o_r.at[q])
        unpack(ob[q, 0:n].astype(F32), 1 - c, q)
        turn_back(1 - c, q)

    steps = {
        "v": step_v, "t": step_t, "r": step_r, "w": step_w,
        "p": step_p, "b": step_b, "pt": step_pt,
        "vs": lambda o: y_send(v_ops, o), "vf": lambda o: y_forward(v_ops, o),
        "ts": lambda o: y_send(t_ops, o), "tf": lambda o: y_forward(t_ops, o),
        "lf": lambda q: ring_forward(tl, tl_r1, tl_s2, tl_r2, q), "l": step_left,
        "mf": lambda q: ring_forward(mb, m_r1, m_s2, m_r2, q), "m": step_mixed,
        "dr": lambda s, q: dot_rest(stages[s], q), "d": lambda s, q, o: dot_main(stages[s], q, o),
        "re": lambda s, q: relay(stages[s], q), "mix": step_mix,
        "fin": step_finish, "col": step_collect,
    }
    for step in SCHEDULE:
        steps[step[0]](*step[1:])
    for ops in (v_ops, t_ops):
        for h in (0, 1):
            exchange(ops, h, False)
    for copy in pending:
        copy.wait_send()


class Ops(NamedTuple):
    p: Any
    m: Any
    r: Any
    x: Any
    as_: Any
    ar: Any
    s1: Any
    r1: Any
    s2: Any
    r2: Any


class Stage(NamedTuple):
    ops: Any
    lhs: Any
    cs: Any
    own: Any
    l1: Any
    l2: Any
    s1: Any
    r1: Any
    s2: Any
    r2: Any


def per_device(pair_count, coupling, amplitudes, integrals):
    dma = pltpu.SemaphoreType.DMA
    coupling, amplitudes, integrals = (jnp.transpose(v, (0, 2, 1)) for v in (coupling, amplitudes, integrals))
    turned, shard = (2, COLS, ROWS), (2, ROWS, COLS)

    def piece(*lead, dtype=BF16):
        return pltpu.VMEM((*lead, PMAX, 128), dtype)

    def right():
        return [
            pltpu.VMEM((2, 2, PV, 128), BF16), pltpu.VMEM((4, 4, 2 * H, 128), BF16), pltpu.VMEM((4, H, 128), BF16),
            pltpu.VMEM((4, RG, 128), BF16), dma((2, 2, 2)), dma((4, 2)),
            dma((2, 5)), dma((2, 5)), dma((2, 5)), dma((2, 5)),
        ]

    def sums():
        return [
            pltpu.VMEM((Q, 2 * RMAX, 1152), BF16), piece(3, 2 * Q), piece(2 * Q, dtype=F32), piece(2, Q), piece(2, 2 * Q),
            dma((2, Q)), dma((2, Q)), dma((2, 2 * Q)), dma((2, 2 * Q)),
        ]

    scratch = [pltpu.VMEM(turned, BF16)] * 3 + [dma((3,)), pltpu.VMEM(turned, BF16)] + [pltpu.VMEM(shard, BF16)] * 3
    scratch += [piece(2, Q), piece(4, 2 * Q), dma((2, 2, Q)), dma((2, 2 * Q)), dma((2, Q)), dma((2, Q)), dma((2, Q))]
    scratch += [piece(2, Q), piece(2 * Q), dma((2, Q))]
    scratch += right() + right()
    scratch += [piece(4, 2 * Q), dma((2, 2 * Q)), dma((2, 2 * Q)), dma((2, Q)), dma((2, Q))]
    scratch += sums() + sums()
    scratch += [piece(2, Q), piece(Q), pltpu.VMEM(shard, BF16), dma((Q,)), dma((Q,))]
    result = pl.pallas_call(
        kernel,
        out_shape=jax.ShapeDtypeStruct(turned, BF16),
        in_specs=[pl.BlockSpec(memory_space=pltpu.SMEM)] + [pl.BlockSpec(memory_space=pl.ANY)] * 3,
        out_specs=pl.BlockSpec(memory_space=pltpu.VMEM),
        scratch_shapes=scratch,
        compiler_params=pltpu.CompilerParams(collective_id=0, has_side_effects=True, vmem_limit_bytes=56 << 20),
        cost_estimate=pl.CostEstimate(flops=6115295232, bytes_accessed=2654208, transcendentals=0),
        name="cycle",
    )(pair_count, coupling, amplitudes, integrals)
    return jnp.transpose(result, (0, 2, 1))


def solution(mesh):
    split = P(None, "row", "col")
    return jax.shard_map(per_device, mesh=mesh, in_specs=(P(), split, split, split), out_specs=split, check_vma=False)
```
